32 devices in a mesh: batch: 4 (over z), token: 8 (over y, x, core).
Axes of the slice: x: 2, y: 2, z: 4, core: 2. Of those that a mesh axis runs over, the one named last changes fastest.
Arguments:
- pooled: bfloat16 [256, 512, 64], P('token', 'batch'), may hold values from -100 to 100
- token_of: int32 [256], P('token'), may hold values from 0 to 15, as said below
- proj: bfloat16 [16, 1024, 2048], P('token'), may hold values from -2 to 2
- w_up: bfloat16 [16, 2048, 8192], P('token', None, 'batch'), may hold values from -0.125 to 0.125
- w_down: bfloat16 [16, 8192, 2048], P('token', 'batch'), may hold values from -0.0625 to 0.0625
- cotangent: bfloat16 [512, 16, 2048], P('batch', 'token'), may hold values from -0.75 to 0.75
Outputs:
- block_out: bfloat16 [512, 16, 2048], P('batch', 'token')
- grad_up: bfloat16 [16, 2048, 8192], P('token', None, 'batch')
- grad_down: bfloat16 [16, 8192, 2048], P('token', 'batch')
The draws below stay inside these ranges and needn't reach their ends.
Inputs may be any that keep to these rules, and one draw needn't show every extreme that they name: `token_of`: in every aligned block of 16 features, each token is named by exactly one feature.
All inputs are finite; a program needn't handle non-finite values.
Results may differ from the reference program's by a relative error of at most 0.015.
Values may be sent and summed in bfloat16 or wider, within the bound.
No kernel may reach another device: no remote copies, remote signals or barrier semaphores. Data moves between devices by JAX's collectives and lax.ppermute only.
A program may use at most 128 MiB of HBM per device.

```python
import jax
import jax.numpy as jnp
from jax import lax

D = 2048
TOKENS = 16
HEADS = 16
FF = 8192
E = 64
HEAD = 128
F = 256
CW = 1024
ROWS = 512
N_BATCH = 4


def spread(key, shape, lower, upper):
    return jnp.exp(jax.random.uniform(key, shape, jnp.float32, jnp.log(lower), jnp.log(upper)))


def permute_block(key):
    return jax.random.permutation(key, TOKENS)


def draw_token_of(key, part):
    key = jax.random.fold_in(key, 11)
    block_keys = jax.random.split(key, F // TOKENS)
    blocks = jax.vmap(permute_block)(block_keys)
    return blocks.reshape(F).astype(jnp.int32)


def draw_pooled(key, part):
    key = jax.random.fold_in(key, 12)
    key_base, key_row, key_col = jax.random.split(key, 3)
    base = jnp.clip(jax.random.normal(key_base, (F, ROWS, E), jnp.float32), -4.0, 4.0)
    return (base * spread(key_row, (1, ROWS, 1), 0.5, 5.0) * spread(key_col, (F, 1, E), 0.5, 5.0)).astype(jnp.bfloat16)


def draw_proj(key, part):
    key = jax.random.fold_in(key, 13)
    key_base, key_col = jax.random.split(key, 2)
    base = jnp.clip(jax.random.normal(key_base, (TOKENS, CW, D), jnp.float32), -4.0, 4.0)
    return (base * CW ** (-0.5) * spread(key_col, (TOKENS, 1, D), 0.5, 5.0)).astype(jnp.bfloat16)


def mixed_tokens(key, part):
    pooled = draw_pooled(key, part)
    token_of = draw_token_of(key, part)
    proj = draw_proj(key, part)
    blocks = F // TOKENS
    lookup = token_of.reshape(blocks, TOKENS)
    targets = jnp.arange(TOKENS, dtype=jnp.int32)
    onehot = (lookup[:, None, :] == targets[None, :, None]).astype(jnp.float32)
    grouped = pooled.reshape(blocks, TOKENS, ROWS, E)
    features = jnp.einsum('ktf,kfre->rtke', onehot, grouped).reshape(ROWS, TOKENS, CW)
    embedded = jnp.einsum('rtc,tcd->rtd', features, proj)
    mixing = jnp.transpose(embedded.reshape(ROWS, TOKENS, HEADS, HEAD), (0, 2, 1, 3)).reshape(ROWS, HEADS, D)
    summed = mixing + embedded
    center = summed - jnp.mean(summed, axis=-1, keepdims=True)
    variance = jnp.mean(center * center, axis=-1, keepdims=True)
    return center / jnp.sqrt(variance + 1e-05)


def draw_cotangent(key, part):
    aligned = mixed_tokens(key, part)
    key = jax.random.fold_in(key, 14)
    noise = 0.05 * jnp.clip(jax.random.normal(key, (ROWS, TOKENS, D), jnp.float32), -4.0, 4.0)
    weight_aligned = 0.05
    return jnp.clip(weight_aligned * aligned + noise, -0.75, 0.75).astype(jnp.bfloat16)


def block_scale(own_key, shape, pieces, least, top_value):
    gain, own = 1.0, jax.random.fold_in(own_key, 6)
    for position, shards_of in pieces:
        heights = jnp.exp(jax.random.uniform(jax.random.fold_in(own, position), (shards_of,), jnp.float32, least / len(pieces), top_value / len(pieces)))
        gain = gain * jnp.repeat(heights, shape[position] // shards_of).reshape([-1 if axis == position else 1 for axis in range(len(shape))])
    return gain


def normal_values(rng, shape, scale, most, cuts=(), kind=jnp.bfloat16):
    array = scale * jax.random.normal(rng, shape, jnp.float32)
    if cuts:
        array = array * block_scale(rng, shape, cuts, -0.22, 0.18)
    return jnp.clip(array, -most, most).astype(kind)


def setup_inputs(seed: int = 0) -> dict:
    key_list = jax.random.split(jax.random.key(seed), 7)
    return {
        "pooled": draw_pooled(jax.random.fold_in(key_list[6], 71), 0),
        "token_of": draw_token_of(jax.random.fold_in(key_list[6], 71), 0),
        "proj": draw_proj(jax.random.fold_in(key_list[6], 71), 0),
        "w_up": normal_values(key_list[3], (TOKENS, D, FF), D ** -0.5, 0.125, ((0, 8), (2, 4))),
        "w_down": normal_values(key_list[4], (TOKENS, FF, D), FF ** -0.5, 0.0625, ((0, 8), (1, 4))),
        "cotangent": draw_cotangent(jax.random.fold_in(key_list[6], 71), 0),
    }


EPSILON = 1e-05

def normalize(values):
    center = values - lax.optimization_barrier(jnp.mean(values, axis=-1, keepdims=True))
    variance = lax.optimization_barrier(jnp.mean(center * center, axis=-1, keepdims=True))
    return center * lax.rsqrt(variance + EPSILON)

def group_sum(act, down_weight):
    grouped_act = act.reshape(act.shape[0], N_BATCH, FF // N_BATCH)
    grouped_down = down_weight.reshape(N_BATCH, FF // N_BATCH, D)

    def one_group(operands):
        act_part, down_part = operands
        partial_value = jnp.dot(act_part, down_part, preferred_element_type=jnp.float32)
        partial_value = lax.optimization_barrier(partial_value.astype(jnp.bfloat16))
        return partial_value.astype(jnp.float32)
    partials = lax.map(one_group, (jnp.transpose(grouped_act, (1, 0, 2)), grouped_down))
    return lax.optimization_barrier(jnp.sum(partials, axis=0))

def per_token(operands):
    normed_tok, up_weight, down_weight, cot_tok = operands
    pre = jnp.dot(normed_tok, up_weight, preferred_element_type=jnp.float32)
    act = jax.nn.gelu(pre).astype(jnp.bfloat16)
    ffn = group_sum(act, down_weight)
    summed = ffn + normed_tok.astype(jnp.float32)
    result, pullback = jax.vjp(normalize, summed)
    back = pullback(cot_tok.astype(jnp.float32))[0].astype(jnp.bfloat16)
    grad_down = jnp.dot(act.T, back, preferred_element_type=jnp.float32).astype(jnp.bfloat16)
    back_hidden = jnp.dot(back, down_weight.T, preferred_element_type=jnp.float32)
    pre_grad = jax.vjp(jax.nn.gelu, pre)[1](back_hidden)[0].astype(jnp.bfloat16)
    grad_up = jnp.dot(normed_tok.T, pre_grad, preferred_element_type=jnp.float32).astype(jnp.bfloat16)
    return (result.astype(jnp.bfloat16), grad_up, grad_down)

def reference(pooled, token_of, proj, w_up, w_down, cotangent):
    blocks = F // TOKENS
    lookup = token_of.reshape(blocks, TOKENS)
    targets = jnp.arange(TOKENS, dtype=jnp.int32)
    onehot = (lookup[:, None, :] == targets[None, :, None]).astype(jnp.float32)
    grouped = pooled.reshape(blocks, TOKENS, ROWS, E).astype(jnp.float32)
    features_cat = jnp.einsum('ktf,kfre->rtke', onehot, grouped).astype(jnp.bfloat16).reshape(ROWS, TOKENS, CW)
    embedded = jnp.einsum('rtc,tcd->rtd', features_cat.astype(jnp.float32), proj.astype(jnp.float32)).astype(jnp.bfloat16)
    mixing = jnp.transpose(embedded.reshape(ROWS, TOKENS, HEADS, HEAD), (0, 2, 1, 3)).reshape(ROWS, HEADS, D)
    normed = normalize(mixing.astype(jnp.float32) + embedded.astype(jnp.float32)).astype(jnp.bfloat16)
    outputs, grad_up, grad_down = lax.map(per_token, (jnp.transpose(normed, (1, 0, 2)), w_up, w_down, jnp.transpose(cotangent, (1, 0, 2))))
    block_out = jnp.transpose(outputs, (1, 0, 2))
    return (block_out, grad_up, grad_down)
```

```python
import functools
import math

import jax
import jax.numpy as jnp
from jax import lax
from jax.experimental import pallas as pl
from jax.experimental.pallas import tpu as pltpu
from jax.sharding import PartitionSpec as P

TOKENS = 16
EPSILON = 1e-05
GRAD_TILES = 8
GELU_C = math.sqrt(2.0 / math.pi)
GELU_A = 0.044715
BF16 = jnp.bfloat16
F32 = jnp.float32
MIB = 1024 * 1024
IN_VMEM = pl.BlockSpec(memory_space=pltpu.VMEM)
ANYWHERE = pl.BlockSpec(memory_space=pl.ANY)


def params(mib):
    return pltpu.CompilerParams(vmem_limit_bytes=mib * MIB)


def cost(flops, moved, trans=0):
    return pl.CostEstimate(flops=flops, bytes_accessed=moved, transcendentals=trans)


def shape(*dims):
    return jax.ShapeDtypeStruct(dims, BF16)


def project_kernel(chips, feats_ref, proj_ref, *refs):
    embedded_ref, sends, (held, sems) = refs[-chips - 3], refs[-chips - 2 : -2], refs[-2:]
    local = feats_ref.shape[2]
    tile = held.shape[3]
    me = lax.axis_index("token")
    starts, copies = [], []
    for k in range(chips):
        start = pl.multiple_of(((me // 2) ^ k) * tile, tile)
        starts.append(start)
        for t in range(local):
            copies.append(
                pltpu.make_async_copy(
                    proj_ref.at[t, :, pl.ds(start, tile)], held.at[k, t], sems.at[k, t]
                )
            )
            copies[-1].start()
    joined = []
    for t in range(local):
        slots = [me ^ source for source in range(2 * chips)]
        joined.append(
            jnp.concatenate([feats_ref[lax.rem(s, 2), s // 2, t] for s in slots], axis=1)
        )
    for k in range(chips):
        for t in range(local):
            copies[k * local + t].wait()
            value = jnp.dot(joined[t], held[k, t], preferred_element_type=F32).astype(BF16)
            embedded_ref[t, :, pl.ds(starts[k], tile)] = value
            sends[k][0, t] = value[:, : tile // 2]
            sends[k][1, t] = value[:, tile // 2 :]


def project(feats, proj, after=()):
    _, chips, local, rows, part = feats.shape
    depth, width = proj.shape[1:]
    tile = width // chips
    return pl.pallas_call(
        functools.partial(project_kernel, chips),
        in_specs=[IN_VMEM] + [ANYWHERE] * (1 + len(after)),
        out_specs=[IN_VMEM] * (chips + 1),
        out_shape=[shape(local, rows, width)] + [shape(2, local, rows, tile // 2)] * chips,
        scratch_shapes=[
            pltpu.VMEM((chips, local, depth, tile), BF16),
            pltpu.SemaphoreType.DMA((chips, local)),
        ],
        compiler_params=params(16),
        cost_estimate=cost(2 * local * rows * depth * width, 2 * local * depth * width),
        name="project",
    )(feats, proj, *after)


def norm_kernel(chips, head, *refs):
    blocks, got_ref, embedded_ref = refs[:chips], refs[chips], refs[chips + 1]
    normed_ref, sum_ref = refs[-2:]
    local = embedded_ref.shape[0]
    me = lax.axis_index("token")
    core = lax.rem(me, 2)
    for k in range(chips):
        for other in range(2):
            source = me ^ (2 * k + other)
            for a in range(local):
                value = got_ref[k, a] if other else blocks[k][core, a]
                start = pl.multiple_of((source * local + a) * head, head)
                columns = pl.ds(start, head)
                for b in range(local):
                    sum_ref[b, :, columns] = value[:, b * head : (b + 1) * head].astype(
                        F32
                    ) + embedded_ref[b, :, columns].astype(F32)
    for b in range(local):
        values = sum_ref[b]
        center = values - jnp.mean(values, axis=-1, keepdims=True)
        variance = jnp.mean(center * center, axis=-1, keepdims=True)
        normed_ref[b] = (center * lax.rsqrt(variance + EPSILON)).astype(BF16)


def norm_mixed(blocks, got, embedded, after=()):
    local, rows, width = embedded.shape
    chips = len(blocks)
    head = width // TOKENS
    tile = min(rows, 64)
    return pl.pallas_call(
        functools.partial(norm_kernel, chips, head),
        grid=(rows // tile,),
        in_specs=[pl.BlockSpec((2, local, tile, local * head), lambda r: (0, 0, r, 0))] * chips
        + [
            pl.BlockSpec((chips, local, tile, local * head), lambda r: (0, 0, r, 0)),
            pl.BlockSpec((local, tile, width), lambda r: (0, r, 0)),
        ]
        + [ANYWHERE] * len(after),
        out_specs=pl.BlockSpec((local, tile, width), lambda r: (0, r, 0)),
        out_shape=shape(local, rows, width),
        scratch_shapes=[pltpu.VMEM((local, tile, width), F32)],
        compiler_params=params(12),
        cost_estimate=cost(10 * local * rows * width, 8 * local * rows * width),
        name="norm_mixed",
    )(*blocks, got, embedded, *after)


def ffn_kernel(token, blocks, tiles, *refs):
    normeds, (up_ref, down_ref) = refs[:blocks], refs[blocks : blocks + 2]
    outs, (up_buf, down_buf, up_sems, down_sems) = refs[-4 - 3 * blocks : -4], refs[-4:]
    slopes, acts, parts = outs[:blocks], outs[blocks : 2 * blocks], outs[2 * blocks :]
    rows = normeds[0].shape[1]
    tile = up_buf.shape[2]
    ups, downs = [], []
    for f in range(tiles):
        hidden = pl.ds(f * tile, tile)
        ups.append(
            pltpu.make_async_copy(up_ref.at[token, :, hidden], up_buf.at[f], up_sems.at[f])
        )
        downs.append(
            pltpu.make_async_copy(down_ref.at[token, hidden, :], down_buf.at[f], down_sems.at[f])
        )
    for copy in ups + downs:
        copy.start()
    normed = jnp.concatenate([ref[0] for ref in normeds], axis=0)
    for f in range(tiles):
        ups[f].wait()
        pre = jnp.dot(normed, up_buf[f], preferred_element_type=F32)
        square = pre * pre
        tanh = jnp.tanh(GELU_C * pre * (1.0 + GELU_A * square))
        half = 0.5 * (1.0 + tanh)
        act = (pre * half).astype(BF16)
        slope = half + (0.5 * GELU_C) * pre * (1.0 - tanh * tanh) * (1.0 + (3.0 * GELU_A) * square)
        slope = slope.astype(BF16)
        for k in range(blocks):
            some = slice(k * rows, (k + 1) * rows)
            acts[k][:, f * tile : (f + 1) * tile] = act[some]
            slopes[k][:, f * tile : (f + 1) * tile] = slope[some]
    total = None
    for f in range(tiles):
        downs[f].wait()
        act = jnp.concatenate([ref[:, f * tile : (f + 1) * tile] for ref in acts], axis=0)
        value = jnp.dot(act, down_buf[f], preferred_element_type=F32)
        total = value if total is None else total + value
    for k in range(blocks):
        parts[k][...] = total[k * rows : (k + 1) * rows].astype(BF16)


def feed_forward(token, normeds, w_up, w_down, after=()):
    blocks = len(normeds)
    rows, width = normeds[0].shape[1:]
    hidden = w_up.shape[2]
    tile = min(hidden, 512)
    tiles = hidden // tile
    outs = pl.pallas_call(
        functools.partial(ffn_kernel, token, blocks, tiles),
        grid=(1,),
        in_specs=[pl.BlockSpec((1, rows, width), lambda i: (token, 0, 0))] * blocks
        + [ANYWHERE] * (2 + len(after)),
        out_specs=[IN_VMEM] * (3 * blocks),
        out_shape=[shape(rows, hidden)] * (2 * blocks) + [shape(rows, width)] * blocks,
        scratch_shapes=[
            pltpu.VMEM((tiles, width, tile), BF16),
            pltpu.VMEM((tiles, tile, width), BF16),
            pltpu.SemaphoreType.DMA((tiles,)),
            pltpu.SemaphoreType.DMA((tiles,)),
        ],
        compiler_params=params(22 + 5 * blocks),
        cost_estimate=cost(
            4 * blocks * rows * width * hidden, 4 * width * hidden, blocks * rows * hidden
        ),
        name="feed_forward",
    )(*normeds, w_up, w_down, *after)
    return [(outs[k], outs[blocks + k], outs[2 * blocks + k]) for k in range(blocks)]


def back_kernel(arrived, *refs):
    part_ref, normed_ref, cot_ref = refs[arrived : arrived + 3]
    out_ref, back_ref = refs[-2:]
    values = part_ref[...].astype(F32)
    for ref in refs[:arrived]:
        values += ref[...].astype(F32)
    values += normed_ref[0].astype(F32)
    center = values - jnp.mean(values, axis=-1, keepdims=True)
    variance = jnp.mean(center * center, axis=-1, keepdims=True)
    scale = lax.rsqrt(variance + EPSILON)
    result = center * scale
    out_ref[...] = result.astype(BF16)
    cot = cot_ref[0].astype(F32)
    mean_cot = jnp.mean(cot, axis=-1, keepdims=True)
    mean_dot = jnp.mean(cot * result, axis=-1, keepdims=True)
    back_ref[...] = (scale * (cot - mean_cot - result * mean_dot)).astype(BF16)


def back_norm(token, arrived, part, normed, cot, after=()):
    rows, width = part.shape
    tile = min(rows, 64)
    flat = pl.BlockSpec((tile, width), lambda r: (r, 0))
    mine = pl.BlockSpec((1, tile, width), lambda r: (token, r, 0))
    return pl.pallas_call(
        functools.partial(back_kernel, len(arrived)),
        grid=(rows // tile,),
        in_specs=[flat] * (len(arrived) + 1) + [mine, mine] + [ANYWHERE] * len(after),
        out_specs=[flat, flat],
        out_shape=[shape(rows, width)] * 2,
        compiler_params=params(10),
        cost_estimate=cost(20 * rows * width, 12 * rows * width),
        name="back_norm",
    )(*arrived, part, normed, cot, *after)


def grad_kernel(blocks, *refs):
    backs, normeds = refs[:blocks], refs[blocks : 2 * blocks]
    slopes, acts = refs[2 * blocks : 3 * blocks], refs[3 * blocks : 4 * blocks]
    down_ref = refs[4 * blocks]
    up_out, down_out, back_all, normed_t = refs[-4:]
    rows = backs[0].shape[0]

    @pl.when(pl.program_id(0) == 0)
    def _():
        for k in range(blocks):
            back_all[k * rows : (k + 1) * rows, :] = backs[k][...]
            normed_t[:, k * rows : (k + 1) * rows] = normeds[k][0].T

    back = back_all[...]
    back_hidden = lax.dot_general(
        back, down_ref[0], (((1,), (1,)), ((), ())), preferred_element_type=F32
    )
    slope = jnp.concatenate([ref[...] for ref in slopes], axis=0)
    pre_grad = (back_hidden * slope.astype(F32)).astype(BF16)
    act = jnp.concatenate([ref[...] for ref in acts], axis=0)
    down_out[0] = lax.dot_general(
        act, back, (((0,), (0,)), ((), ())), preferred_element_type=F32
    ).astype(BF16)
    up_out[0] = jnp.dot(normed_t[...], pre_grad, preferred_element_type=F32).astype(BF16)


def weight_grads(token, first, count, backs, normeds, slopes, acts, w_down, earlier, after=()):
    blocks = len(backs)
    rows, width = backs[0].shape
    local, hidden = w_down.shape[:2]
    tile = hidden // GRAD_TILES
    whole = pl.BlockSpec((rows, width), lambda f: (0, 0))
    mine = pl.BlockSpec((1, rows, width), lambda f: (token, 0, 0))
    columns = pl.BlockSpec((rows, tile), lambda f: (0, first + f))
    down_spec = pl.BlockSpec((1, tile, width), lambda f: (token, first + f, 0))
    up_spec = pl.BlockSpec((1, width, tile), lambda f: (token, 0, first + f))
    place = 4 * blocks + 1
    return pl.pallas_call(
        functools.partial(grad_kernel, blocks),
        grid=(count,),
        in_specs=[whole] * blocks
        + [mine] * blocks
        + [columns] * (2 * blocks)
        + [down_spec]
        + [ANYWHERE] * (len(earlier) + len(after)),
        out_specs=[up_spec, down_spec],
        out_shape=[shape(local, width, hidden), shape(local, hidden, width)],
        scratch_shapes=[
            pltpu.VMEM((blocks * rows, width), BF16),
            pltpu.VMEM((width, blocks * rows), BF16),
        ],
        input_output_aliases={place + i: i for i in range(len(earlier))},
        compiler_params=params(40),
        cost_estimate=cost(
            6 * blocks * rows * width * tile * count, 6 * width * tile * count, 0
        ),
        name="weight_grads",
    )(*backs, *normeds, *slopes, *acts, w_down, *earlier, *after)


def per_device(batch_size, token_size, pooled, token_of, proj, w_up, w_down, cotangent):
    chips = token_size // 2
    local = proj.shape[0]
    core = lax.rem(lax.axis_index("token"), 2)
    chip = lax.axis_index("token") // 2
    right = [(i, (i + 1) % batch_size) for i in range(batch_size)]
    swap = [(d, d ^ 1) for d in range(token_size)]

    def onward(value):
        return lax.ppermute(value, "batch", right)

    local_feats, rows, feat_width = pooled.shape
    blocks = local_feats // TOKENS
    lookup = token_of.reshape(blocks, TOKENS)
    targets = jnp.arange(TOKENS, dtype=jnp.int32)
    onehot = (lookup[:, None, :] == targets[None, :, None]).astype(BF16)
    grouped = pooled.reshape(blocks, TOKENS, rows, feat_width)
    ordered = jnp.concatenate(
        [
            jnp.einsum("tf,fre->tre", onehot[k], grouped[k], preferred_element_type=F32).astype(BF16)
            for k in range(blocks)
        ],
        axis=2,
    ).reshape(chips, 2, local, rows, blocks * feat_width)

    def exchange(shift):
        parts = []
        for k in range(chips):
            part = lax.dynamic_index_in_dim(ordered, chip ^ k, 0, False)
            if k or shift:
                pairs = [
                    (z * token_size + d, (z + shift) % batch_size * token_size + (d ^ (2 * k)))
                    for z in range(batch_size)
                    for d in range(token_size)
                ]
                part = lax.ppermute(part, ("batch", "token"), pairs)
            parts.append(part)
        mine = jnp.stack([lax.dynamic_index_in_dim(p, core, 0, False) for p in parts])
        other = jnp.stack([lax.dynamic_index_in_dim(p, 1 - core, 0, False) for p in parts])
        return jnp.stack([mine, lax.ppermute(other, "token", swap)])

    feats = [None, exchange(1)]
    feats[0] = exchange(0)
    for k in range(2, batch_size):
        feats.append(onward(feats[-1]))

    def mixing_parts(sends):
        parts = [sends[0]]
        for k in range(1, chips):
            pairs = [(d, d ^ (2 * k)) for d in range(token_size)]
            parts.append(lax.ppermute(sends[k], "token", pairs))
        other = jnp.stack([lax.dynamic_index_in_dim(p, 1 - core, 0, False) for p in parts])
        return parts, lax.ppermute(other, "token", swap)

    cot = jnp.transpose(cotangent, (1, 0, 2))
    last = []
    embedded, mixed, normed, forward = {}, {}, {}, {}

    def run_project(k):
        embedded[k], *sends = project(feats[k], proj, last)
        last[:] = [embedded[k]]
        mixed[k] = mixing_parts(sends)

    def run_norm(k):
        normed[k] = norm_mixed(*mixed[k], embedded[k], last)
        last[:] = [normed[k]]

    def run_ffn(t, ks):
        done = feed_forward(t, [normed[k] for k in ks], w_up, w_down, last)
        last[:] = [done[0][2]]
        for k, value in zip(ks, done):
            forward[k, t] = value

    end = batch_size - 1
    run_project(1)
    run_project(0)
    run_project(2)
    run_norm(1)
    for t in range(local):
        run_ffn(t, [1])
    for k in range(2, end):
        run_project(k + 1)
        run_norm(k)
        for t in range(local):
            run_ffn(t, [k])
    run_norm(end)
    run_norm(0)
    for t in range(local):
        run_ffn(t, [end, 0])

    outs, backs = [], []
    sums = [forward[1, t][2] for t in range(local)]
    for k in range(2, batch_size):
        for t in range(local):
            sums[t] = (onward(sums[t]).astype(F32) + forward[k, t][2].astype(F32)).astype(BF16)
    for t in range(local):
        out, back = back_norm(t, [onward(sums[t])], forward[0, t][2], normed[0], cot, last)
        last[:] = [out]
        outs.append(out)
        backs.append([back])
    for k in range(1, batch_size):
        for t in range(local):
            backs[t].append(onward(backs[t][-1]))

    grads = []
    for t in range(local):
        grads = weight_grads(
            t,
            0,
            GRAD_TILES,
            backs[t],
            [normed[k] for k in range(batch_size)],
            [forward[k, t][0] for k in range(batch_size)],
            [forward[k, t][1] for k in range(batch_size)],
            w_down,
            grads,
            last,
        )
    return (jnp.stack(outs, axis=1), grads[0], grads[1])


def solution(mesh):
    in_specs = (
        P("token", "batch", None),
        P("token"),
        P("token", None, None),
        P("token", None, "batch"),
        P("token", "batch", None),
        P("batch", "token", None),
    )
    out_specs = (P("batch", "token", None), P("token", None, "batch"), P("token", "batch", None))
    return jax.shard_map(
        functools.partial(per_device, mesh.shape["batch"], mesh.shape["token"]),
        mesh=mesh,
        in_specs=in_specs,
        out_specs=out_specs,
        check_vma=False,
    )
```

```python
import functools
import math

import jax
import jax.numpy as jnp
from jax import lax
from jax.experimental import pallas as pl
from jax.experimental.pallas import tpu as pltpu
from jax.sharding import PartitionSpec as P

TOKENS = 16
EPSILON = 1e-05
GRAD_TILES = 8
GELU_C = math.sqrt(2.0 / math.pi)
GELU_A = 0.044715
BF16 = jnp.bfloat16
F32 = jnp.float32
MIB = 1024 * 1024
BRIEF = pl.CostEstimate(flops=1, bytes_accessed=1, transcendentals=0)
IN_HBM = pl.BlockSpec(memory_space=pltpu.HBM)
IN_VMEM = pl.BlockSpec(memory_space=pltpu.VMEM)
ANYWHERE = pl.BlockSpec(memory_space=pl.ANY)


def params(mib):
    return pltpu.CompilerParams(vmem_limit_bytes=mib * MIB)


def shape(*dims):
    return jax.ShapeDtypeStruct(dims, BF16)


def project_kernel(chips, blocks, *refs):
    feats, proj_ref = refs[:blocks], refs[blocks]
    embedded_ref, sends = refs[-chips - 1], refs[-chips:]
    sources, local = feats[0].shape[:2]
    tile = proj_ref.shape[2] // chips
    chip = lax.axis_index("token") // 2
    for t in range(local):
        joined = jnp.concatenate(
            [
                jnp.concatenate([ref[s, t] for s in range(sources)], axis=1)
                for ref in feats
            ],
            axis=0,
        )
        for k in range(chips):
            columns = pl.ds(pl.multiple_of((chip ^ k) * tile, tile), tile)
            value = jnp.dot(joined, proj_ref[t, :, columns], preferred_element_type=F32)
            value = value.astype(BF16)
            embedded_ref[t, :, columns] = value
            sends[k][0, t] = value[:, : tile // 2]
            sends[k][1, t] = value[:, tile // 2 :]


def project(feats, proj, after=()):
    blocks = len(feats)
    sources, local, rows, _ = feats[0].shape
    rows *= blocks
    chips = sources // 2
    width = proj.shape[2]
    tile = width // chips
    return pl.pallas_call(
        functools.partial(project_kernel, chips, blocks),
        in_specs=[IN_VMEM] * (blocks + 1) + [ANYWHERE] * len(after),
        out_specs=[IN_VMEM] * (chips + 1),
        out_shape=[shape(local, rows, width)] + [shape(2, local, rows, tile // 2)] * chips,
        compiler_params=params(14 + 4 * blocks),
        cost_estimate=BRIEF,
        name="project",
    )(*feats, proj, *after)


def other_kernel(chips, *refs):
    core = lax.rem(lax.axis_index("token"), 2)
    for k in range(chips):
        refs[-1][k] = refs[k][1 - core]


def for_other_core(parts, after=()):
    chips = len(parts)
    return pl.pallas_call(
        functools.partial(other_kernel, chips),
        in_specs=[IN_VMEM] * chips + [ANYWHERE] * len(after),
        out_specs=IN_VMEM,
        out_shape=shape(chips, *parts[0].shape[1:]),
        compiler_params=params(8),
        cost_estimate=BRIEF,
        name="for_other_core",
    )(*parts, *after)


def norm_kernel(chips, head, *refs):
    blocks, got_ref, embedded_ref = refs[:chips], refs[chips], refs[chips + 1]
    normed_ref, sum_ref = refs[-2:]
    local = embedded_ref.shape[0]
    me = lax.axis_index("token")
    core = lax.rem(me, 2)
    for k in range(chips):
        for other in range(2):
            source = me ^ (2 * k + other)
            for a in range(local):
                value = got_ref[k, a] if other else blocks[k][core, a]
                start = pl.multiple_of((source * local + a) * head, head)
                columns = pl.ds(start, head)
                for b in range(local):
                    sum_ref[b, :, columns] = value[:, b * head : (b + 1) * head].astype(
                        F32
                    ) + embedded_ref[b, :, columns].astype(F32)
    for b in range(local):
        values = sum_ref[b]
        center = values - jnp.mean(values, axis=-1, keepdims=True)
        variance = jnp.mean(center * center, axis=-1, keepdims=True)
        normed_ref[b] = (center * lax.rsqrt(variance + EPSILON)).astype(BF16)


def norm_mixed(blocks, got, embedded, after=()):
    local, rows, width = embedded.shape
    chips = len(blocks)
    head = width // TOKENS
    tile = min(rows, 64)
    return pl.pallas_call(
        functools.partial(norm_kernel, chips, head),
        grid=(rows // tile,),
        in_specs=[pl.BlockSpec((2, local, tile, local * head), lambda r: (0, 0, r, 0))] * chips
        + [
            pl.BlockSpec((chips, local, tile, local * head), lambda r: (0, 0, r, 0)),
            pl.BlockSpec((local, tile, width), lambda r: (0, r, 0)),
        ]
        + [ANYWHERE] * len(after),
        out_specs=pl.BlockSpec((local, tile, width), lambda r: (0, r, 0)),
        out_shape=shape(local, rows, width),
        scratch_shapes=[pltpu.VMEM((local, tile, width), F32)],
        compiler_params=params(12),
        cost_estimate=BRIEF,
        name="norm_mixed",
    )(*blocks, got, embedded, *after)


def ffn_kernel(token, tiles, normed_ref, up_ref, down_ref, *refs):
    slope_ref, act_ref, part_ref, up_buf, down_buf, up_sems, down_sems = refs[-7:]
    slots, _, tile = up_buf.shape
    ups, downs = [], []
    for f in range(tiles):
        hidden = pl.ds(f * tile, tile)
        slot = f % slots
        ups.append(
            pltpu.make_async_copy(up_ref.at[token, :, hidden], up_buf.at[slot], up_sems.at[slot])
        )
        downs.append(
            pltpu.make_async_copy(down_ref.at[token, hidden, :], down_buf.at[f], down_sems.at[f])
        )
    for copy in ups[:slots] + downs:
        copy.start()
    for f in range(tiles):
        columns = slice(f * tile, (f + 1) * tile)
        ups[f].wait()
        pre = jnp.dot(normed_ref[0], up_buf[f % slots], preferred_element_type=F32)
        if f + slots < tiles:
            ups[f + slots].start()
        square = pre * pre
        tanh = jnp.tanh(GELU_C * pre * (1.0 + GELU_A * square))
        half = 0.5 * (1.0 + tanh)
        act_ref[:, columns] = (pre * half).astype(BF16)
        slope = half + (0.5 * GELU_C) * pre * (1.0 - tanh * tanh) * (1.0 + (3.0 * GELU_A) * square)
        slope_ref[:, columns] = slope.astype(BF16)
    total = None
    for f in range(tiles):
        downs[f].wait()
        act = act_ref[:, f * tile : (f + 1) * tile]
        value = jnp.dot(act, down_buf[f], preferred_element_type=F32)
        total = value if total is None else total + value
    part_ref[...] = total.astype(BF16)


def feed_forward(token, normed, w_up, w_down, after=()):
    rows, width = normed.shape[1:]
    hidden = w_up.shape[2]
    tile = min(hidden, 512)
    tiles = hidden // tile
    return pl.pallas_call(
        functools.partial(ffn_kernel, token, tiles),
        grid=(1,),
        in_specs=[pl.BlockSpec((1, rows, width), lambda i: (token, 0, 0))]
        + [ANYWHERE] * (2 + len(after)),
        out_specs=[IN_VMEM] * 3,
        out_shape=[shape(rows, hidden)] * 2 + [shape(rows, width)],
        scratch_shapes=[
            pltpu.VMEM((min(tiles, 2), width, tile), BF16),
            pltpu.VMEM((tiles, tile, width), BF16),
            pltpu.SemaphoreType.DMA((min(tiles, 2),)),
            pltpu.SemaphoreType.DMA((tiles,)),
        ],
        compiler_params=params(16 + rows // 25),
        cost_estimate=BRIEF,
        name="feed_forward",
    )(normed, w_up, w_down, *after)


def back_kernel(arrived, *refs):
    part_ref, normed_ref, cot_ref = refs[arrived : arrived + 3]
    out_ref, back_ref = refs[-2:]
    values = part_ref[...].astype(F32)
    for ref in refs[:arrived]:
        values += ref[...].astype(F32)
    values += normed_ref[0].astype(F32)
    center = values - jnp.mean(values, axis=-1, keepdims=True)
    variance = jnp.mean(center * center, axis=-1, keepdims=True)
    scale = lax.rsqrt(variance + EPSILON)
    result = center * scale
    out_ref[...] = result.astype(BF16)
    cot = cot_ref[0].astype(F32)
    mean_cot = jnp.mean(cot, axis=-1, keepdims=True)
    mean_dot = jnp.mean(cot * result, axis=-1, keepdims=True)
    back_ref[...] = (scale * (cot - mean_cot - result * mean_dot)).astype(BF16)


def back_norm(token, arrived, part, normed, cot, after=()):
    rows, width = arrived[0].shape
    tile = min(rows, 64)
    ahead = (part.shape[0] - rows) // tile
    flat = pl.BlockSpec((tile, width), lambda r: (r, 0))
    own = pl.BlockSpec((tile, width), lambda r: (ahead + r, 0))
    mine = pl.BlockSpec((1, tile, width), lambda r: (token, r, 0))
    mine_last = pl.BlockSpec((1, tile, width), lambda r: (token, ahead + r, 0))
    return pl.pallas_call(
        functools.partial(back_kernel, len(arrived)),
        grid=(rows // tile,),
        in_specs=[flat] * len(arrived) + [own, mine_last, mine] + [ANYWHERE] * len(after),
        out_specs=[flat, flat],
        out_shape=[shape(rows, width)] * 2,
        compiler_params=params(10),
        cost_estimate=BRIEF,
        name="back_norm",
    )(*arrived, part, normed, cot, *after)


def add_kernel(arrived_ref, part_ref, *refs):
    rows = arrived_ref.shape[0]
    total = arrived_ref[...].astype(F32) + part_ref[:rows, :].astype(F32)
    refs[-1][...] = total.astype(BF16)


def add(arrived, part, after=()):
    return pl.pallas_call(
        add_kernel,
        in_specs=[IN_VMEM] * 2 + [ANYWHERE] * len(after),
        out_specs=IN_VMEM,
        out_shape=shape(*arrived.shape),
        compiler_params=params(8),
        cost_estimate=BRIEF,
        name="add",
    )(arrived, part, *after)


def hold_kernel(value_ref, *refs):
    refs[-1][...] = value_ref[...]


def hold(value, after):
    return pl.pallas_call(
        hold_kernel,
        in_specs=[IN_VMEM] + [ANYWHERE] * len(after),
        out_specs=IN_VMEM,
        out_shape=shape(*value.shape),
        compiler_params=params(8),
        cost_estimate=BRIEF,
        name="hold",
    )(value, *after)


def load_kernel(proj_ref, *refs):
    held, sems = refs[-2:]
    copies = [
        pltpu.make_async_copy(proj_ref.at[t], held.at[t], sems.at[t]) for t in range(held.shape[0])
    ]
    for copy in copies:
        copy.start()
    for copy in copies:
        copy.wait()


def load(proj, after=()):
    return pl.pallas_call(
        load_kernel,
        in_specs=[ANYWHERE] * (1 + len(after)),
        out_specs=IN_VMEM,
        out_shape=shape(*proj.shape),
        scratch_shapes=[pltpu.SemaphoreType.DMA((proj.shape[0],))],
        compiler_params=params(10),
        cost_estimate=pl.CostEstimate(flops=1, bytes_accessed=4 * proj.size, transcendentals=0),
        name="load",
    )(proj, *after)


def transpose_kernel(groups, token, *refs):
    start = 0
    for k in range(groups):
        stop = start + refs[k].shape[1]
        refs[-1][:, start:stop] = refs[k][token].T
        start = stop


def transposed(token, normeds, after=()):
    groups = len(normeds)
    width = normeds[0].shape[2]
    rows = sum(normed.shape[1] for normed in normeds)
    return pl.pallas_call(
        functools.partial(transpose_kernel, groups, token),
        in_specs=[IN_VMEM] * groups + [ANYWHERE] * len(after),
        out_specs=IN_VMEM,
        out_shape=shape(width, rows),
        compiler_params=params(12),
        cost_estimate=BRIEF,
        name="transposed",
    )(*normeds, *after)


def grad_kernel(blocks, groups, token, first, *refs):
    backs, refs = refs[:blocks], refs[blocks:]
    slopes, acts, refs = refs[:groups], refs[groups : 2 * groups], refs[2 * groups :]
    normed_t, down_ref = refs[:2]
    up_out, down_out, back_all, held, sems = refs[-5:]
    rows = backs[0].shape[0]
    tile = held.shape[1]
    step = pl.program_id(0)

    def fetch(index):
        hidden = pl.ds(pl.multiple_of((first + index) * tile, tile), tile)
        slot = lax.rem(index, 2)
        return pltpu.make_async_copy(down_ref.at[token, hidden, :], held.at[slot], sems.at[slot])

    @pl.when(step == 0)
    def _():
        fetch(step).start()

    @pl.when(step + 1 < pl.num_programs(0))
    def _():
        fetch(step + 1).start()

    @pl.when(step == 0)
    def _():
        for k in range(blocks):
            back_all[k * rows : (k + 1) * rows, :] = backs[k][...]

    back = back_all[...]
    fetch(step).wait()
    back_hidden = lax.dot_general(
        back, held[lax.rem(step, 2)], (((1,), (1,)), ((), ())), preferred_element_type=F32
    )
    slope = jnp.concatenate([ref[...] for ref in slopes], axis=0)
    pre_grad = (back_hidden * slope.astype(F32)).astype(BF16)
    act = jnp.concatenate([ref[...] for ref in acts], axis=0)
    down_out[0] = lax.dot_general(
        act, back, (((0,), (0,)), ((), ())), preferred_element_type=F32
    ).astype(BF16)
    up_out[0] = jnp.dot(normed_t[...], pre_grad, preferred_element_type=F32).astype(BF16)


def weight_grads(token, first, count, backs, slopes, acts, normed_t, w_down, earlier, after=()):
    blocks, groups = len(backs), len(acts)
    rows, width = backs[0].shape
    local, hidden = w_down.shape[:2]
    tile = hidden // GRAD_TILES
    columns = [pl.BlockSpec((act.shape[0], tile), lambda f: (0, first + f)) for act in acts]
    down_spec = pl.BlockSpec((1, tile, width), lambda f: (token, first + f, 0))
    up_spec = pl.BlockSpec((1, width, tile), lambda f: (token, 0, first + f))
    place = blocks + 2 * groups + 2
    return pl.pallas_call(
        functools.partial(grad_kernel, blocks, groups, token, first),
        grid=(count,),
        in_specs=[IN_VMEM] * blocks
        + columns * 2
        + [IN_VMEM, IN_HBM]
        + [ANYWHERE] * (len(earlier) + len(after)),
        out_specs=[up_spec, down_spec],
        out_shape=[shape(local, width, hidden), shape(local, hidden, width)],
        scratch_shapes=[
            pltpu.VMEM((blocks * rows, width), BF16),
            pltpu.VMEM((2, tile, width), BF16),
            pltpu.SemaphoreType.DMA((2,)),
        ],
        input_output_aliases={place + i: i for i in range(len(earlier))},
        compiler_params=params(28),
        cost_estimate=pl.CostEstimate(
            flops=6 * blocks * rows * width * tile * count,
            bytes_accessed=6 * width * tile * count,
            transcendentals=0,
        ),
        name="weight_grads",
    )(*backs, *slopes, *acts, normed_t, w_down, *earlier, *after)


def per_device(batch_size, token_size, pooled, token_of, proj, w_up, w_down, cotangent):
    chips = token_size // 2
    local = proj.shape[0]
    right = [(i, (i + 1) % batch_size) for i in range(batch_size)]
    swap = [(d, d ^ 1) for d in range(token_size)]

    def onward(value, what):
        with jax.named_scope(what):
            return lax.ppermute(value, "batch", right)

    local_feats, rows, feat_width = pooled.shape
    blocks = local_feats // TOKENS
    lookup = token_of.reshape(blocks, TOKENS)
    targets = jnp.arange(TOKENS, dtype=jnp.int32)
    onehot = (lookup[:, None, :] == targets[None, :, None]).astype(BF16)
    grouped = pooled.reshape(blocks, TOKENS, rows, feat_width)
    ordered = jnp.concatenate(
        [
            jnp.einsum("tf,fre->tre", onehot[k], grouped[k], preferred_element_type=F32).astype(BF16)
            for k in range(blocks)
        ],
        axis=2,
    ).reshape(token_size, local, rows, blocks * feat_width)

    feats = [lax.all_to_all(ordered, "token", split_axis=0, concat_axis=0, tiled=True)]
    for k in range(1, batch_size):
        feats.append(onward(feats[-1], f"features_{k}"))

    cot = jnp.transpose(cotangent, (1, 0, 2))
    last = []
    embedded, parts, normed, forward = {}, {}, {}, {}

    end = batch_size - 1
    groups = [(k,) for k in range(1, end)] + [(end, 0)]

    def run_project(g):
        embedded[g], *sends = project([feats[k] for k in groups[g]], proj, last)
        last[:] = [embedded[g]]
        parts[g] = [sends[0]]
        for chip in range(1, chips):
            pairs = [(d, d ^ (2 * chip)) for d in range(token_size)]
            with jax.named_scope(f"heads_{g}_{chip}"):
                parts[g].append(lax.ppermute(sends[chip], "token", pairs))

    def run_swap(g):
        other = for_other_core(parts[g], last)
        last[:] = [other]
        with jax.named_scope(f"core_{g}"):
            parts[g] = parts[g], lax.ppermute(other, "token", swap)

    def run_norm(g):
        normed[g] = norm_mixed(*parts[g], embedded[g], last)
        last[:] = [normed[g]]

    def run_ffn(t, g):
        forward[g, t] = feed_forward(t, normed[g], w_up, w_down, last)
        last[:] = [forward[g, t][2]]

    def run_back(t, arrived):
        out, back = back_norm(t, arrived, forward[final, t][2], normed[final], cot, last)
        last[:] = [out]
        return out, back

    def run_grads(t, first, count, backs, turned, earlier):
        grads = weight_grads(
            t,
            first,
            count,
            backs[1:] + backs[:1],
            [forward[g, t][0] for g in order],
            [forward[g, t][1] for g in order],
            turned,
            w_down,
            earlier,
            last,
        )
        last[:] = []
        return grads

    final = len(groups) - 1
    order = list(range(len(groups)))
    sums = [None] * local

    def run_sum(t, g):
        part = forward[g, t][2]
        total = part[:rows] if g == 0 else add(sums[t], part, last)
        if g:
            last[:] = [total]
        sums[t] = onward(total, f"sum_{t}_{g + 1}")

    proj = load(proj, [feats[0]])
    run_project(0)
    run_swap(0)
    if final > 0:
        run_project(1)
    for g in order:
        run_norm(g)
        for t in range(local):
            run_ffn(t, g)
            run_sum(t, g)
            if g == t == 0 and final:
                run_swap(1)
        if 0 < g < final:
            last.append(sums[0])
            run_swap(g + 1)
        if g + 2 <= final:
            run_project(g + 2)
    turned = []
    for t in range(local):
        turned.append(transposed(t, [normed[g] for g in order], last))
        last[:] = [turned[-1]]

    outs, backs = [], []
    for t in range(local):
        out, back = run_back(t, [sums[t]])
        outs.append(out)
        if t:
            back = hold(back, [backs[0][end - 1]])
        backs.append([back])
        for k in range(1, batch_size):
            backs[t].append(onward(backs[t][-1], f"back_{t}_{k}"))

    grads = []
    first = GRAD_TILES // 2
    for t in range(local - 1):
        grads = run_grads(t, 0, first, backs[t], turned[t], grads)
        last[:] = [backs[t + 1][end - 1]]
        grads = run_grads(t, first, GRAD_TILES - first, backs[t], turned[t], grads)
    grads = run_grads(local - 1, 0, GRAD_TILES, backs[-1], turned[-1], grads)
    return (jnp.stack(outs, axis=1), grads[0], grads[1])


def solution(mesh):
    in_specs = (
        P("token", "batch", None),
        P("token"),
        P("token", None, None),
        P("token", None, "batch"),
        P("token", "batch", None),
        P("batch", "token", None),
    )
    out_specs = (P("batch", "token", None), P("token", None, "batch"), P("token", "batch", None))
    return jax.shard_map(
        functools.partial(per_device, mesh.shape["batch"], mesh.shape["token"]),
        mesh=mesh,
        in_specs=in_specs,
        out_specs=out_specs,
        check_vma=False,
    )
```
